32 devices in a mesh: groups: 2 (over x), cand: 16 (over z, y, core).
Axes of the slice: x: 2, y: 2, z: 4, core: 2. Of those that a mesh axis runs over, the one named last changes fastest.
Arguments:
- cand_rows: bfloat16 [24576, 1024], P(('groups', 'cand')), parts along dimension 0, may hold values from -6 to 6
- user_rows: bfloat16 [192, 1024], P(('groups', 'cand')), parts along dimension 0, may hold values from -6 to 6
- counts: int32 [192], P(('groups', 'cand')), parts along dimension 0, may hold values from 16 to 512, as said below
- starts: int32 [192], P(('groups', 'cand')), parts along dimension 0, may hold values from 0 to 47, as said below
- norm_gain: float32 [1024], replicated, may hold values from 0.1 to 1.9
- w_cand: bfloat16 [1024, 1024], replicated, may hold values from -0.1875 to 0.1875
- w_user: bfloat16 [1024, 1024], replicated, may hold values from -0.1875 to 0.1875
- w_query: bfloat16 [1024, 1024], replicated, may hold values from -0.25 to 0.25
- w_key: bfloat16 [1024, 1024], replicated, may hold values from -0.25 to 0.25
- w_value: bfloat16 [1024, 1024], replicated, may hold values from -0.1875 to 0.1875
- w_out: bfloat16 [1024, 1024], replicated, may hold values from -0.1875 to 0.1875
- w_score: float32 [1024], replicated, may hold values from -0.1875 to 0.1875
Outputs:
- score: float32 [24576], P(('groups', 'cand')), parts along dimension 0
The draws below stay inside these ranges and needn't reach their ends.
There are 2 independent parts, one for each index of `groups`. The reference program is written for one: setup_inputs(seed, part) draws one part's arguments, and reference() takes and returns one part's arrays. A program takes and returns all parts, laid end to end along the dimension named above; an argument that names none is the same for every part. Nothing has to cross between parts.
Inputs may be any that keep to these rules, and one draw needn't show every extreme that they name: Within a shard the requests' first tiles increase. Each request's tiles run from its first tile to the next request's first tile; for a shard's last request, to the shard's end and then through the next shard's tiles before that shard's first request. On shard 0 the first request starts at tile 0, elsewhere at most 8 tiles in, which some shard reaches; the last shard's last request ends with the shard and starts at its last tile. `counts`: each count is at most the rows of its request's tiles; some request has exactly 512.
All inputs are finite; a program needn't handle non-finite values.
Results may differ from the reference program's by a relative error of at most 0.0045.
Values may be sent and summed in bfloat16 or wider, within the bound.
A program may use at most 128 MiB of HBM per device.

```python
import jax
import jax.numpy as jnp
from jax import lax

D = 1024
HEADS = 8
CAND_DEV = 768
REQ_DEV = 6
TILE = 16
MAXC = 512
MINC = 16
SPILL = 128
TOTAL = 12288
REQS = 96
N_CAND = 16


def layout(key):
    shards = N_CAND
    tiles = CAND_DEV // TILE
    long_tiles = MAXC // TILE
    spill_tiles = SPILL // TILE
    key = jax.random.fold_in(key, 7)
    keys = jax.random.split(key, 4)
    shard_ids = jnp.arange(shards, dtype=jnp.int32)
    spill_in = jax.random.randint(keys[0], (shards,), 0, spill_tiles + 1)
    forced = jax.random.randint(keys[1], (), 1, shards)
    spill_in = jnp.where(shard_ids == forced, spill_tiles, spill_in)
    spill_in = jnp.where(shard_ids == 0, 0, spill_in).astype(jnp.int32)
    spill_out = jnp.concatenate([spill_in[1:], jnp.zeros((1,), jnp.int32)])
    heavy_shard = jax.random.randint(keys[2], (), 0, shards)

    def one_shard(shard_key, s_in, s_out, shard):
        sub = jax.random.split(shard_key, 4)
        avail = tiles - long_tiles - s_in
        tile_ids = jnp.arange(tiles, dtype=jnp.int32)
        raw = jax.random.randint(sub[0], (tiles,), 0, 1 << 20)
        ranking = jnp.where((tile_ids >= 1) & (tile_ids < avail), raw * tiles + tile_ids, -1 - tile_ids)
        is_last = shard == shards - 1
        ranking = jnp.where(is_last & (tile_ids == avail - 1), 1 << 30, ranking)
        picked = lax.top_k(ranking, REQ_DEV - 1)[1].astype(jnp.int32)
        cuts = jnp.sort(picked)
        relative = jnp.concatenate([jnp.zeros((1,), jnp.int32), cuts])
        long_any = jax.random.randint(sub[1], (), 0, REQ_DEV)
        long_early = jax.random.randint(sub[3], (), 0, REQ_DEV - 1)
        long_index = jnp.where(is_last, long_early, long_any)
        slots = jnp.arange(REQ_DEV, dtype=jnp.int32)
        firsts = relative + s_in + long_tiles * (slots > long_index).astype(jnp.int32)
        ends = jnp.concatenate([firsts[1:], (tiles + s_out)[None]])
        span = (ends - firsts) * TILE
        amounts = jax.random.randint(sub[2], (REQ_DEV,), MINC, jnp.minimum(span, MAXC) + 1)
        amounts = jnp.where((shard == heavy_shard) & (slots == long_index), MAXC, amounts)
        return (firsts.astype(jnp.int32), amounts.astype(jnp.int32))
    firsts, amounts = jax.vmap(one_shard)(jax.random.split(keys[3], shards), spill_in, spill_out, shard_ids)
    return (firsts.reshape(-1), amounts.reshape(-1))


def draw_counts(key, part):
    return layout(key)[1]


def draw_starts(key, part):
    return layout(key)[0]


def draw_cand_rows(key, part):
    key = jax.random.fold_in(key, 11)
    keys = jax.random.split(key, 3)
    rows = jax.random.normal(keys[2], (TOTAL, D), jnp.float32)
    return jnp.clip(rows, -6.0, 6.0).astype(jnp.bfloat16)


def paired_weights(key):
    key = jax.random.fold_in(key, 23)
    keys = jax.random.split(key, 2)
    base = jax.random.normal(keys[0], (D, D), jnp.float32)
    extra = jax.random.normal(keys[1], (D, D), jnp.float32)
    limit = 8.0 * D ** (-0.5)
    scale = D ** (-0.5)
    query_weight = base * scale
    key_weight = extra * scale
    return (jnp.clip(query_weight, -limit, limit), jnp.clip(key_weight, -limit, limit))


def draw_w_query(key, part):
    return paired_weights(key)[0].astype(jnp.bfloat16)


def draw_w_key(key, part):
    return paired_weights(key)[1].astype(jnp.bfloat16)


def steps_of(own_key, extent, pieces, smallest, largest):
    level, own = 1.0, jax.random.fold_in(own_key, 6)
    for dim, parts in pieces:
        steps = jnp.exp(jax.random.uniform(jax.random.fold_in(own, dim), (parts,), jnp.float32, smallest / len(pieces), largest / len(pieces)))
        level = level * jnp.repeat(steps, extent[dim] // parts).reshape([-1 if axis == dim else 1 for axis in range(len(extent))])
    return level


def bell_draw(stream_key, extent, deviation, most, cuts=(), kind=jnp.bfloat16):
    gain = steps_of(stream_key, extent, cuts, -0.22, 0.18) if cuts else 1.0
    values = jax.random.normal(stream_key, extent, jnp.float32) * deviation * gain
    return jnp.minimum(jnp.maximum(values, -most), most).astype(kind)


def setup_inputs(seed: int = 0, part: int = 0) -> dict:
    splits = jax.random.split(jax.random.key(seed), 13)
    part_keys = jax.random.split(jax.random.fold_in(splits[12], part), 13)
    cand_rows = draw_cand_rows(jax.random.fold_in(jax.random.fold_in(splits[12], part), 71), part)
    user_rows = bell_draw(part_keys[1], (REQS, D), 1.0, 6.0, ((0, 16),))
    counts = draw_counts(jax.random.fold_in(jax.random.fold_in(splits[12], part), 71), part)
    starts = draw_starts(jax.random.fold_in(jax.random.fold_in(splits[12], part), 71), part)
    norm_gain = jnp.clip(1.0 + 0.18 * jax.random.normal(splits[4], (D,), jnp.float32), 0.1, 1.9)
    w_cand = bell_draw(splits[5], (D, D), D ** -0.5, 0.1875)
    w_user = bell_draw(splits[6], (D, D), D ** -0.5, 0.1875)
    w_query = draw_w_query(jax.random.fold_in(splits[12], 71), part)
    w_key = draw_w_key(jax.random.fold_in(splits[12], 71), part)
    w_value = bell_draw(splits[9], (D, D), D ** -0.5, 0.1875)
    w_out = bell_draw(splits[10], (D, D), D ** -0.5, 0.1875)
    w_score = bell_draw(splits[11], (D,), D ** -0.5, 0.1875, (), jnp.float32)
    return dict(cand_rows=cand_rows, user_rows=user_rows, counts=counts, starts=starts, norm_gain=norm_gain, w_cand=w_cand, w_user=w_user, w_query=w_query, w_key=w_key, w_value=w_value, w_out=w_out, w_score=w_score)


def attend(queries, q_labels, key_rows, value_rows, k_labels, head_count):
    head_size = queries.shape[1] // head_count
    allowed = (q_labels[:, None] == k_labels[None, :]) & (q_labels[:, None] >= 0)

    def one_head(head_index):
        col_start = head_index * head_size
        q_part = lax.dynamic_slice_in_dim(queries, col_start, head_size, 1)
        k_part = lax.dynamic_slice_in_dim(key_rows, col_start, head_size, 1)
        v_part = lax.dynamic_slice_in_dim(value_rows, col_start, head_size, 1)
        scores = lax.dot_general(q_part, k_part, (((1,), (1,)), ((), ())), preferred_element_type=jnp.float32)
        scores = jnp.where(allowed, scores * head_size ** (-0.5), -1e+30)
        row_max = lax.optimization_barrier(jnp.max(scores, axis=1, keepdims=True))
        weights = jnp.exp(scores - row_max)
        row_sum = lax.optimization_barrier(jnp.sum(weights, axis=1, keepdims=True))
        softmax_weights = (weights / row_sum).astype(jnp.bfloat16)
        return jnp.dot(softmax_weights, v_part, preferred_element_type=jnp.float32).astype(jnp.bfloat16)
    mixture = lax.map(one_head, jnp.arange(head_count))
    return jnp.transpose(mixture, (1, 0, 2)).reshape(queries.shape[0], head_count * head_size)

def reference(cand_rows, user_rows, counts, starts, norm_gain, w_cand, w_user, w_query, w_key, w_value, w_out, w_score):
    shards = N_CAND
    user_term = jnp.dot(user_rows, w_user, preferred_element_type=jnp.float32).astype(jnp.bfloat16)
    first_grid = (starts * TILE).reshape(shards, REQ_DEV)
    count_grid = counts.reshape(shards, REQ_DEV)
    term_grid = user_term.reshape(shards, REQ_DEV, D)
    prev_first = jnp.concatenate([jnp.zeros((1,), jnp.int32), first_grid[:-1, -1]])
    prev_count = jnp.concatenate([jnp.zeros((1,), jnp.int32), count_grid[:-1, -1]])
    prev_term = jnp.concatenate([jnp.zeros((1, D), jnp.bfloat16), term_grid[:-1, -1]])

    def prepare(inputs):
        block, firsts, amounts, terms, p_first, p_count, p_term = inputs
        position = jnp.arange(CAND_DEV, dtype=jnp.int32)
        holder = lax.optimization_barrier(jnp.sum((position[:, None] >= firsts[None, :]).astype(jnp.int32), axis=1)) - 1
        chosen = holder[:, None] == jnp.arange(REQ_DEV, dtype=jnp.int32)[None, :]
        row_first = lax.optimization_barrier(jnp.sum(jnp.where(chosen, firsts[None, :], 0), axis=1))
        row_count = lax.optimization_barrier(jnp.sum(jnp.where(chosen, amounts[None, :], 0), axis=1))
        usable = jnp.where(holder >= 0, position - row_first < row_count, position + CAND_DEV - p_first < p_count)
        labels = jnp.where(usable, holder + 1, -1)
        user_sel = jnp.dot(chosen.astype(jnp.bfloat16), terms, preferred_element_type=jnp.float32)
        user_sel = user_sel + jnp.where(holder[:, None] < 0, p_term[None, :].astype(jnp.float32), 0.0)
        features = block.astype(jnp.float32)
        mean_square = lax.optimization_barrier(jnp.mean(features * features, axis=1, keepdims=True))
        normed = (features * lax.rsqrt(mean_square + 1e-06) * norm_gain[None, :]).astype(jnp.bfloat16)
        pre_act = jnp.dot(normed, w_cand, preferred_element_type=jnp.float32) + user_sel
        hidden = (features + jax.nn.silu(pre_act)).astype(jnp.bfloat16)
        queries = jnp.dot(hidden, w_query, preferred_element_type=jnp.float32).astype(jnp.bfloat16)
        key_rows = jnp.dot(hidden, w_key, preferred_element_type=jnp.float32).astype(jnp.bfloat16)
        value_rows = jnp.dot(hidden, w_value, preferred_element_type=jnp.float32).astype(jnp.bfloat16)
        return (hidden, queries, jnp.concatenate([key_rows, value_rows], axis=1), labels, usable)
    blocks = cand_rows.reshape(shards, CAND_DEV, D)
    hidden, queries, key_value, labels, usable = lax.map(prepare, (blocks, first_grid, count_grid, term_grid, prev_first, prev_count, prev_term))
    lower_rim = jnp.concatenate([jnp.zeros((1, MAXC, 2 * D), jnp.bfloat16), key_value[:-1, CAND_DEV - MAXC:]], axis=0)
    upper_rim = jnp.concatenate([key_value[1:, :MAXC], jnp.zeros((1, MAXC, 2 * D), jnp.bfloat16)], axis=0)

    def finish(inputs):
        hid, qry, kval, low, upp, labs, keep, firsts, amounts, p_first, p_count = inputs
        offsets = jnp.arange(MAXC, dtype=jnp.int32)
        lower_pos = CAND_DEV - MAXC + offsets - p_first
        lower_labels = jnp.where((lower_pos >= 0) & (lower_pos < p_count), 0, -1)
        upper_labels = jnp.where(CAND_DEV + offsets - firsts[REQ_DEV - 1] < amounts[REQ_DEV - 1], REQ_DEV, -1)
        key_labels = jnp.concatenate([lower_labels, labs, upper_labels])
        widened = jnp.concatenate([low, kval, upp], axis=0)
        mixture = attend(qry, labs, widened[:, :D], widened[:, D:], key_labels, HEADS)
        mixture = jnp.where(keep[:, None], mixture, jnp.zeros_like(mixture))
        combined = hid.astype(jnp.float32) + jnp.dot(mixture, w_out, preferred_element_type=jnp.float32)
        score = lax.optimization_barrier(jnp.sum(combined * w_score[None, :], axis=1))
        return jnp.where(keep, score, 0.0)
    scores = lax.map(finish, (hidden, queries, key_value, lower_rim, upper_rim, labels, usable, first_grid, count_grid, prev_first, prev_count))
    return scores.reshape(TOTAL)
```

```python
import functools
import math

import jax
import jax.numpy as jnp
from jax import lax
from jax.experimental import pallas as pl
from jax.experimental.pallas import tpu as pltpu
from jax.sharding import PartitionSpec as P

HEADS = 8
TILE = 16
SPILL = 128
MAXC = 512
LANES = 128
FAR = -1e30
LOW = 16
MESH = pl.DeviceIdType.MESH


def dot(a, b):
    return jnp.dot(a, b, preferred_element_type=jnp.float32)


def dot_t(a, b):
    return lax.dot_general(
        a, b, (((1,), (1,)), ((), ())), preferred_element_type=jnp.float32
    )


def parts_of(value):
    high = value.astype(jnp.bfloat16)
    return high, (value - high.astype(jnp.float32)).astype(jnp.bfloat16)


def fold_lanes(value):
    total = value[:, :LANES]
    for at in range(LANES, value.shape[1], LANES):
        total = total + value[:, at : at + LANES]
    return total


def kernel(
    shards,
    starts,
    counts,
    x_hbm,
    users,
    gain,
    w_score,
    w_user_hbm,
    w_cand_hbm,
    w_out_hbm,
    w_value_hbm,
    w_query_hbm,
    w_key_hbm,
    out,
    x_own,
    x_next,
    w_user,
    w_cand,
    w_out,
    w_value,
    w_query,
    w_key,
    terms,
    hidden,
    queries,
    keys,
    q_mark,
    k_mark,
    sides,
    total,
    score_out,
    score_in,
    load_sem,
    send_sem,
    recv_sem,
):
    local, width = x_own.shape
    reqs = starts.shape[0]
    head_size = width // HEADS
    rows_all = local + SPILL
    me = lax.axis_index("cand")
    has_lower = me > 0
    has_upper = me < shards - 1

    loads = []
    pairs = (
        (x_hbm, x_own),
        (w_user_hbm, w_user),
        (w_cand_hbm, w_cand),
        (w_out_hbm, w_out),
        (w_value_hbm, w_value),
        (w_query_hbm, w_query),
        (w_key_hbm, w_key),
    )
    for at, (src, dst) in enumerate(pairs):
        copy = pltpu.make_async_copy(src, dst, load_sem.at[at])
        copy.start()
        loads.append(copy)

    barrier = pltpu.get_barrier_semaphore()

    @pl.when(has_lower)
    def _():
        pl.semaphore_signal(barrier, inc=1, device_id={"cand": me - 1}, device_id_type=MESH)

    @pl.when(has_upper)
    def _():
        pl.semaphore_signal(barrier, inc=1, device_id={"cand": me + 1}, device_id_type=MESH)

    def rows_down():
        return pltpu.make_async_remote_copy(
            src_ref=x_hbm.at[pl.ds(0, SPILL)],
            dst_ref=x_next,
            send_sem=send_sem.at[0],
            recv_sem=recv_sem.at[0],
            device_id={"cand": me - 1},
            device_id_type=MESH,
        )

    def score_up():
        return pltpu.make_async_remote_copy(
            src_ref=score_out,
            dst_ref=score_in,
            send_sem=send_sem.at[1],
            recv_sem=recv_sem.at[1],
            device_id={"cand": me + 1},
            device_id_type=MESH,
        )

    lane = lax.broadcasted_iota(jnp.int32, (1, LANES), 1)
    first = jnp.full((1, LANES), 1 << 28, jnp.int32)
    after = jnp.full((1, LANES), 1 << 28, jnp.int32)
    live_end = jnp.zeros((1, LANES), jnp.int32)
    for j in range(reqs):
        row = starts[j] * TILE
        first = jnp.where(lane == j, row, first)
        live_end = jnp.where(lane == j, row + counts[j], live_end)
        if j:
            after = jnp.where(lane == j - 1, row, after)

    def marks(base, rows):
        place = base + lax.broadcasted_iota(jnp.int32, (rows, LANES), 0)
        held = (place >= first) & (place < after)
        live = (place >= first) & (place < live_end)
        return held, live

    for base in range(0, rows_all, SPILL):
        _, live = marks(base, SPILL)
        live_f = jnp.where(live, 1.0, 0.0)
        dead = 1.0 - jnp.sum(live_f, axis=1, keepdims=True)
        q_mark[pl.ds(base, SPILL), :] = jnp.where(live, 0.0, FAR).astype(jnp.bfloat16)
        k_mark[pl.ds(base, SPILL), :] = jnp.where(
            lane == LANES - 1, dead, live_f
        ).astype(jnp.bfloat16)

    terms[...] = jnp.zeros_like(terms)
    loads[1].wait()
    terms[0:reqs, :] = dot(users[...], w_user[...])

    both = jnp.where(has_lower, 1, 0) + jnp.where(has_upper, 1, 0)
    pl.semaphore_wait(barrier, both)

    @pl.when(has_lower)
    def _():
        rows_down().start()

    @pl.when(jnp.logical_not(has_upper))
    def _():
        x_next[...] = jnp.zeros_like(x_next)

    @pl.when(jnp.logical_not(has_lower))
    def _():
        score_in[...] = jnp.zeros_like(score_in)

    def pointwise(base, rows, x):
        features = x.astype(jnp.float32)
        mean_square = jnp.mean(features * features, axis=1, keepdims=True)
        normed = (features * lax.rsqrt(mean_square + 1e-06) * gain[...]).astype(jnp.bfloat16)
        held, _ = marks(base, rows)
        user = dot(jnp.where(held, 1.0, 0.0).astype(jnp.bfloat16), terms[...].astype(jnp.bfloat16))
        pre = dot(normed, w_cand[...]) + user
        silu = pre * (0.5 + 0.5 * jnp.tanh(0.5 * pre))
        hidden[pl.ds(base, rows), :] = (features + silu).astype(jnp.bfloat16)

    loads[0].wait()
    loads[2].wait()
    step = 2 * SPILL
    for base in range(0, local, step):
        pointwise(base, step, x_own[pl.ds(base, step), :])

    loads[3].wait()
    loads[4].wait()
    score_high, rest = parts_of(w_score[...])
    score_mid, score_low = parts_of(w_score[...] - score_high.astype(jnp.float32))
    row_id = lax.broadcasted_iota(jnp.int32, (LANES, width), 0)
    spread = jnp.where(
        row_id == 0,
        score_high.astype(jnp.float32),
        jnp.where(
            row_id == 1,
            score_mid.astype(jnp.float32),
            jnp.where(row_id == 2, score_low.astype(jnp.float32), 0.0),
        ),
    ).astype(jnp.bfloat16)
    u = jnp.sum(dot_t(w_out[...], spread), axis=1, keepdims=True)
    u_high = u.astype(jnp.bfloat16).astype(jnp.float32)
    u_low = u - u_high
    head_of = lax.broadcasted_iota(jnp.int32, (width, LANES), 0) // head_size
    lane_w = lax.broadcasted_iota(jnp.int32, (width, LANES), 1)
    by_head = jnp.where(
        lane_w == head_of, u_high, jnp.where(lane_w == head_of + LOW, u_low, 0.0)
    ).astype(jnp.bfloat16)
    g = dot(w_value[...], by_head)
    g = jnp.where(lane < HEADS, g + pltpu.roll(g, LANES - LOW, 1), 0.0)
    g_high = g.astype(jnp.bfloat16).astype(jnp.float32)
    g_parts = (g_high + pltpu.roll(g - g_high, LOW, 1)).astype(jnp.bfloat16)

    scale = math.log2(math.e) * head_size ** (-0.5)

    def project(base, rows):
        at = pl.ds(base, rows)
        block = hidden[at, :]
        q = (dot(block, w_query[...]) * scale).astype(jnp.bfloat16)
        for h in range(HEADS):
            queries[h, at, :] = q[:, h * head_size : (h + 1) * head_size]
        k = dot(block, w_key[...]).astype(jnp.bfloat16)
        for h in range(HEADS):
            keys[h, at, :] = k[:, h * head_size : (h + 1) * head_size]
        v = dot(block, g_parts)
        v = jnp.where(lane < HEADS, v + pltpu.roll(v, LANES - LOW, 1), 0.0)
        v_high = v.astype(jnp.bfloat16).astype(jnp.float32)
        sides[at, :LANES] = (v_high + pltpu.roll(v - v_high, LOW, 1)).astype(jnp.bfloat16)
        sides[at, LANES:] = jnp.ones((rows, LANES), jnp.bfloat16)
        total[at, :] = fold_lanes(block.astype(jnp.float32) * w_score[...])

    loads[5].wait()
    loads[6].wait()
    for base in range(0, local, step):
        project(base, step)

    @pl.when(has_upper)
    def _():
        rows_down().wait_recv()

    @pl.when(has_lower)
    def _():
        rows_down().wait_send()

    pointwise(local, SPILL, x_next[...])
    project(local, SPILL)

    def attend(h, base, rows):
        reach = MAXC - TILE
        low = max(0, base - reach) // SPILL * SPILL
        high = min(rows_all, -(-(base + rows + reach) // SPILL) * SPILL)
        at, span = pl.ds(base, rows), pl.ds(low, high - low)
        q = jnp.concatenate([queries[h, at, :], q_mark[at, :]], axis=1)
        k = jnp.concatenate([keys[h, span, :], k_mark[span, :]], axis=1)
        s = dot_t(q, k)
        p = jnp.exp2(s - jnp.max(s, axis=1, keepdims=True)).astype(jnp.bfloat16)
        o = dot(p, sides[span, :])
        mine = (lane == h) | (lane == h + LOW)
        total[at, :] += jnp.where(mine, o[:, :LANES] / o[:, LANES:], 0.0)

    def scores(base, rows):
        value = jnp.sum(total[pl.ds(base, rows), :].T, axis=0, keepdims=True)
        place = base + lax.broadcasted_iota(jnp.int32, (1, rows), 1)
        live = place < 0
        for j in range(reqs):
            row = starts[j] * TILE
            live = live | ((place >= row) & (place < row + counts[j]))
        return jnp.where(live, value, 0.0), place

    def over_spill(h, carry):
        attend(h, local, SPILL)
        return carry

    lax.fori_loop(0, HEADS, over_spill, 0)
    value, _ = scores(local, SPILL)
    score_out[...] = jnp.broadcast_to(value, score_out.shape)

    @pl.when(has_upper)
    def _():
        score_up().start()

    def over_own(h, carry):
        for base in range(0, local, step):
            attend(h, base, step)
        return carry

    lax.fori_loop(0, HEADS, over_own, 0)
    value, place = scores(0, local)
    out[...] = value

    @pl.when(has_lower)
    def _():
        score_up().wait_recv()

    @pl.when(has_upper)
    def _():
        score_up().wait_send()

    out[:, :SPILL] = jnp.where(
        place[:, :SPILL] < starts[0] * TILE, score_in[0:1, :], value[:, :SPILL]
    )


def per_device(
    shards,
    cand_rows,
    user_rows,
    counts,
    starts,
    norm_gain,
    w_cand,
    w_user,
    w_query,
    w_key,
    w_value,
    w_out,
    w_score,
):
    local, width = cand_rows.shape
    rows_all = local + SPILL
    weight = pltpu.VMEM((width, width), jnp.bfloat16)
    in_smem = pl.BlockSpec(memory_space=pltpu.SMEM)
    in_vmem = pl.BlockSpec(memory_space=pltpu.VMEM)
    anywhere = pl.BlockSpec(memory_space=pl.ANY)
    score = pl.pallas_call(
        functools.partial(kernel, shards),
        out_shape=jax.ShapeDtypeStruct((1, local), jnp.float32),
        in_specs=[in_smem, in_smem, anywhere] + [in_vmem] * 3 + [anywhere] * 6,
        out_specs=in_vmem,
        scratch_shapes=[
            pltpu.VMEM((local, width), jnp.bfloat16),
            pltpu.VMEM((SPILL, width), jnp.bfloat16),
            weight,
            weight,
            weight,
            weight,
            weight,
            weight,
            pltpu.VMEM((LANES, width), jnp.float32),
            pltpu.VMEM((rows_all, width), jnp.bfloat16),
            pltpu.VMEM((HEADS, rows_all, width // HEADS), jnp.bfloat16),
            pltpu.VMEM((HEADS, rows_all, width // HEADS), jnp.bfloat16),
            pltpu.VMEM((rows_all, LANES), jnp.bfloat16),
            pltpu.VMEM((rows_all, LANES), jnp.bfloat16),
            pltpu.VMEM((rows_all, 2 * LANES), jnp.bfloat16),
            pltpu.VMEM((rows_all, LANES), jnp.float32),
            pltpu.VMEM((8, SPILL), jnp.float32),
            pltpu.VMEM((8, SPILL), jnp.float32),
            pltpu.SemaphoreType.DMA((7,)),
            pltpu.SemaphoreType.DMA((2,)),
            pltpu.SemaphoreType.DMA((2,)),
        ],
        compiler_params=pltpu.CompilerParams(
            collective_id=0, has_side_effects=True, vmem_limit_bytes=56 * 1024 * 1024
        ),
        name="rank",
    )(
        starts,
        counts,
        cand_rows,
        user_rows,
        norm_gain[None, :],
        w_score[None, :],
        w_user,
        w_cand,
        w_out,
        w_value,
        w_query,
        w_key,
    )
    return score.reshape(local)


def solution(mesh):
    rows = P(("groups", "cand"))
    wide = P(("groups", "cand"), None)
    return jax.shard_map(
        functools.partial(per_device, mesh.shape["cand"]),
        mesh=mesh,
        in_specs=(wide, wide, rows, rows) + (P(),) * 8,
        out_specs=rows,
        check_vma=False,
    )
```

```python
import functools
import math

import jax
import jax.numpy as jnp
from jax import lax
from jax.experimental import pallas as pl
from jax.experimental.pallas import tpu as pltpu
from jax.sharding import PartitionSpec as P

HEADS = 8
TILE = 16
SPILL = 128
MAXC = 512
LANES = 128
FAR = -1e30
LOW = 16
WIDE = 256
SIDES = 32
MESH = pl.DeviceIdType.MESH


def dot(a, b):
    return jnp.dot(a, b, preferred_element_type=jnp.float32)


def dot_t(a, b):
    return lax.dot_general(
        a, b, (((1,), (1,)), ((), ())), preferred_element_type=jnp.float32
    )


def parts_of(value):
    high = value.astype(jnp.bfloat16)
    return high, (value - high.astype(jnp.float32)).astype(jnp.bfloat16)


def fold_lanes(value):
    total = value[:, :LANES]
    for at in range(LANES, value.shape[1], LANES):
        total = total + value[:, at : at + LANES]
    return total


def kernel(
    shards,
    starts,
    counts,
    x_hbm,
    users,
    gain,
    w_score,
    w_user_hbm,
    w_cand_hbm,
    w_out_hbm,
    w_value_hbm,
    w_query_hbm,
    w_key_hbm,
    out,
    x_own,
    x_next,
    w_user,
    w_cand,
    w_out,
    w_value,
    w_query,
    w_key,
    terms,
    normed,
    hidden,
    queries,
    keys,
    q_mark,
    k_mark,
    sides,
    total,
    mixed,
    score_out,
    score_in,
    load_sem,
    send_sem,
    recv_sem,
):
    local, width = x_own.shape
    reqs = starts.shape[0]
    head_size = width // HEADS
    rows_all = local + SPILL
    me = lax.axis_index("cand")
    has_lower = me > 0
    has_upper = me < shards - 1

    loads = []
    pairs = (
        (x_hbm, x_own),
        (w_user_hbm, w_user),
        (w_cand_hbm, w_cand),
        (w_out_hbm, w_out),
        (w_value_hbm, w_value),
        (w_query_hbm, w_query),
        (w_key_hbm, w_key),
    )
    for at, (src, dst) in enumerate(pairs):
        copy = pltpu.make_async_copy(src, dst, load_sem.at[at])
        copy.start()
        loads.append(copy)

    barrier = pltpu.get_barrier_semaphore()

    @pl.when(has_lower)
    def _():
        pl.semaphore_signal(barrier, inc=1, device_id={"cand": me - 1}, device_id_type=MESH)

    @pl.when(has_upper)
    def _():
        pl.semaphore_signal(barrier, inc=1, device_id={"cand": me + 1}, device_id_type=MESH)

    def rows_down():
        return pltpu.make_async_remote_copy(
            src_ref=x_hbm.at[pl.ds(0, SPILL)],
            dst_ref=x_next,
            send_sem=send_sem.at[0],
            recv_sem=recv_sem.at[0],
            device_id={"cand": me - 1},
            device_id_type=MESH,
        )

    def score_up():
        return pltpu.make_async_remote_copy(
            src_ref=score_out,
            dst_ref=score_in,
            send_sem=send_sem.at[1],
            recv_sem=recv_sem.at[1],
            device_id={"cand": me + 1},
            device_id_type=MESH,
        )

    lane = lax.broadcasted_iota(jnp.int32, (1, LANES), 1)
    first = jnp.full((1, LANES), 1 << 28, jnp.int32)
    after = jnp.full((1, LANES), 1 << 28, jnp.int32)
    live_end = jnp.zeros((1, LANES), jnp.int32)
    for j in range(reqs):
        row = starts[j] * TILE
        first = jnp.where(lane == j, row, first)
        live_end = jnp.where(lane == j, row + counts[j], live_end)
        if j:
            after = jnp.where(lane == j - 1, row, after)

    def marks(base, rows):
        place = base + lax.broadcasted_iota(jnp.int32, (rows, LANES), 0)
        held = (place >= first) & (place < after)
        live = (place >= first) & (place < live_end)
        return held, live

    for base in range(0, rows_all, SPILL):
        _, live = marks(base, SPILL)
        live_f = jnp.where(live, 1.0, 0.0)
        dead = 1.0 - jnp.sum(live_f, axis=1, keepdims=True)
        q_mark[pl.ds(base, SPILL), :] = jnp.where(live, 0.0, FAR).astype(jnp.bfloat16)
        k_mark[pl.ds(base, SPILL), :] = jnp.where(
            lane == LANES - 1, dead, live_f
        ).astype(jnp.bfloat16)

    def normalise(base, rows, x):
        features = x.astype(jnp.float32)
        mean_square = jnp.mean(features * features, axis=1, keepdims=True)
        normed[pl.ds(base, rows), :] = (
            features * lax.rsqrt(mean_square + 1e-06) * gain[...]
        ).astype(jnp.bfloat16)

    loads[0].wait()
    for base in range(0, local, SPILL):
        normalise(base, SPILL, x_own[pl.ds(base, SPILL), :])

    terms[...] = jnp.zeros_like(terms)
    loads[1].wait()
    terms[0:reqs, :] = dot(users[...], w_user[...])

    both = jnp.where(has_lower, 1, 0) + jnp.where(has_upper, 1, 0)
    pl.semaphore_wait(barrier, both)

    @pl.when(has_lower)
    def _():
        rows_down().start()

    @pl.when(jnp.logical_not(has_upper))
    def _():
        x_next[...] = jnp.zeros_like(x_next)

    @pl.when(jnp.logical_not(has_lower))
    def _():
        score_in[...] = jnp.zeros_like(score_in)

    def pointwise(base, rows, x_ref):
        at = pl.ds(base, rows)
        held, _ = marks(base, rows)
        held = jnp.where(held, 1.0, 0.0).astype(jnp.bfloat16)
        for column in range(0, width, WIDE):
            cut = pl.ds(column, WIDE)
            pre = dot(normed[at, :], w_cand[:, cut])
            pre = pre + dot(held, terms[:, cut].astype(jnp.bfloat16))
            silu = pre * (0.5 + 0.5 * jnp.tanh(0.5 * pre))
            hidden[at, cut] = (x_ref[:, cut].astype(jnp.float32) + silu).astype(jnp.bfloat16)

    loads[2].wait()
    step = 2 * SPILL
    pointwise(0, local, x_own)

    loads[3].wait()
    loads[4].wait()
    score_high, rest = parts_of(w_score[...])
    score_mid, score_low = parts_of(w_score[...] - score_high.astype(jnp.float32))
    row_id = lax.broadcasted_iota(jnp.int32, (LANES, width), 0)
    spread = jnp.where(
        row_id == 0,
        score_high.astype(jnp.float32),
        jnp.where(
            row_id == 1,
            score_mid.astype(jnp.float32),
            jnp.where(row_id == 2, score_low.astype(jnp.float32), 0.0),
        ),
    ).astype(jnp.bfloat16)
    u = jnp.sum(dot_t(w_out[...], spread), axis=1, keepdims=True)
    u_high = u.astype(jnp.bfloat16).astype(jnp.float32)
    u_low = u - u_high
    head_of = lax.broadcasted_iota(jnp.int32, (width, LANES), 0) // head_size
    lane_w = lax.broadcasted_iota(jnp.int32, (width, LANES), 1)
    by_head = jnp.where(
        lane_w == head_of, u_high, jnp.where(lane_w == head_of + LOW, u_low, 0.0)
    ).astype(jnp.bfloat16)
    g = dot(w_value[...], by_head)
    g = jnp.where(lane < HEADS, g + pltpu.roll(g, LANES - LOW, 1), 0.0)
    g_high = g.astype(jnp.bfloat16).astype(jnp.float32)
    g_parts = (g_high + pltpu.roll(g - g_high, LOW, 1)).astype(jnp.bfloat16)

    scale = math.log2(math.e) * head_size ** (-0.5)

    def project(weight, kept, base, rows, factor):
        at = pl.ds(base, rows)
        for column in range(0, width, WIDE):
            value = dot(hidden[at, :], weight[:, pl.ds(column, WIDE)])
            value = (value * factor if factor else value).astype(jnp.bfloat16)
            for part in range(0, WIDE, head_size):
                kept[(column + part) // head_size, at, :] = value[:, part : part + head_size]

    def project_side(base, rows):
        at = pl.ds(base, rows)
        block = hidden[at, :]
        v = dot(block, g_parts)
        v = v.T
        v = v[:HEADS] + v[LOW : LOW + HEADS]
        v_high = v.astype(jnp.bfloat16).astype(jnp.float32)
        ones = jnp.ones((SIDES - 2 * HEADS, rows), jnp.float32)
        sides[:, at] = jnp.concatenate([v_high, v - v_high, ones], axis=0).astype(jnp.bfloat16)
        total[at, :] = fold_lanes(block.astype(jnp.float32) * w_score[...])

    loads[5].wait()
    project(w_query, queries, 0, local, scale)
    project_side(0, local)

    @pl.when(has_upper)
    def _():
        rows_down().wait_recv()

    @pl.when(has_lower)
    def _():
        rows_down().wait_send()

    normalise(local, SPILL, x_next[...])
    pointwise(local, SPILL, x_next)
    loads[6].wait()
    project(w_query, queries, local, SPILL, scale)
    project(w_key, keys, 0, rows_all, None)
    project_side(local, SPILL)

    def attend(h, base, rows):
        reach = MAXC - TILE
        low = max(0, base - reach) // SPILL * SPILL
        high = min(rows_all, -(-(base + rows + reach) // SPILL) * SPILL)
        at, span = pl.ds(base, rows), pl.ds(low, high - low)
        q = jnp.concatenate([queries[h, at, :], q_mark[at, :]], axis=1)
        k = jnp.concatenate([keys[h, span, :], k_mark[span, :]], axis=1)
        s = dot_t(k, q)
        p = jnp.exp2(s - jnp.max(s, axis=0, keepdims=True)).astype(jnp.bfloat16)
        o = dot(sides[:, span], p)
        row = lax.broadcasted_iota(jnp.int32, (SIDES, rows), 0)
        mine = (row == h) | (row == h + HEADS)
        above = jnp.sum(jnp.where(mine, o, 0.0), axis=0, keepdims=True)
        mixed[h, :, at] = above / o[2 * HEADS : 2 * HEADS + 1, :]

    def scores(base, rows):
        at = pl.ds(base, rows)
        value = jnp.sum(total[at, :].T, axis=0, keepdims=True)
        for h in range(HEADS):
            value = value + mixed[h, :, at]
        place = base + lax.broadcasted_iota(jnp.int32, (1, rows), 1)
        live = place < 0
        for j in range(reqs):
            row = starts[j] * TILE
            live = live | ((place >= row) & (place < row + counts[j]))
        return jnp.where(live, value, 0.0), place

    def both_kinds(i, carry):
        attend(2 * i, local, SPILL)
        attend(2 * i + 1, local, SPILL)
        for base in range(0, local, step):
            attend(i, base, step)
        return carry

    lax.fori_loop(0, HEADS // 2, both_kinds, 0)
    value, _ = scores(local, SPILL)
    score_out[...] = jnp.broadcast_to(value, score_out.shape)

    @pl.when(has_upper)
    def _():
        score_up().start()

    def own_only(i, carry):
        for base in range(0, local, step):
            attend(HEADS // 2 + 2 * i, base, step)
            attend(HEADS // 2 + 2 * i + 1, base, step)
        return carry

    lax.fori_loop(0, HEADS // 4, own_only, 0)
    value, place = scores(0, local)

    @pl.when(has_lower)
    def _():
        score_up().wait_recv()

    @pl.when(has_upper)
    def _():
        score_up().wait_send()

    head = jnp.where(place[:, :SPILL] < starts[0] * TILE, score_in[0:1, :], value[:, :SPILL])
    out[...] = jnp.concatenate([head, value[:, SPILL:]], axis=1)[0]


def per_device(
    shards,
    cand_rows,
    user_rows,
    counts,
    starts,
    norm_gain,
    w_cand,
    w_user,
    w_query,
    w_key,
    w_value,
    w_out,
    w_score,
):
    local, width = cand_rows.shape
    rows_all = local + SPILL
    weight = pltpu.VMEM((width, width), jnp.bfloat16)
    in_smem = pl.BlockSpec(memory_space=pltpu.SMEM)
    in_vmem = pl.BlockSpec(memory_space=pltpu.VMEM)
    anywhere = pl.BlockSpec(memory_space=pl.ANY)
    return pl.pallas_call(
        functools.partial(kernel, shards),
        out_shape=jax.ShapeDtypeStruct((local,), jnp.float32),
        in_specs=[in_smem, in_smem, anywhere] + [in_vmem] * 3 + [anywhere] * 6,
        out_specs=in_vmem,
        scratch_shapes=[
            pltpu.VMEM((local, width), jnp.bfloat16),
            pltpu.VMEM((SPILL, width), jnp.bfloat16),
            weight,
            weight,
            weight,
            weight,
            weight,
            weight,
            pltpu.VMEM((LANES, width), jnp.float32),
            pltpu.VMEM((rows_all, width), jnp.bfloat16),
            pltpu.VMEM((rows_all, width), jnp.bfloat16),
            pltpu.VMEM((HEADS, rows_all, width // HEADS), jnp.bfloat16),
            pltpu.VMEM((HEADS, rows_all, width // HEADS), jnp.bfloat16),
            pltpu.VMEM((rows_all, LANES), jnp.bfloat16),
            pltpu.VMEM((rows_all, LANES), jnp.bfloat16),
            pltpu.VMEM((SIDES, rows_all), jnp.bfloat16),
            pltpu.VMEM((rows_all, LANES), jnp.float32),
            pltpu.VMEM((HEADS, 1, rows_all), jnp.float32),
            pltpu.VMEM((8, SPILL), jnp.float32),
            pltpu.VMEM((8, SPILL), jnp.float32),
            pltpu.SemaphoreType.DMA((7,)),
            pltpu.SemaphoreType.DMA((2,)),
            pltpu.SemaphoreType.DMA((2,)),
        ],
        compiler_params=pltpu.CompilerParams(
            collective_id=0, has_side_effects=True, vmem_limit_bytes=56 * 1024 * 1024
        ),
        name="rank",
    )(
        starts,
        counts,
        cand_rows,
        user_rows,
        norm_gain[None, :],
        w_score[None, :],
        w_user,
        w_cand,
        w_out,
        w_value,
        w_query,
        w_key,
    )


def solution(mesh):
    rows = P(("groups", "cand"))
    wide = P(("groups", "cand"), None)
    return jax.shard_map(
        functools.partial(per_device, mesh.shape["cand"]),
        mesh=mesh,
        in_specs=(wide, wide, rows, rows) + (P(),) * 8,
        out_specs=rows,
        check_vma=False,
    )
```
